256 devices in a mesh: seq: 32 (over z, x_lo, core), head: 8 (over x_hi, y).
Axes of the slice: x: 4 (x_hi: 2, x_lo: 2; x = x_hi * 2 + x_lo), y: 4, z: 8, core: 2. Of those that a mesh axis runs over, the one named last changes fastest.
Arguments:
- self_queries: bfloat16 [8192, 5120], P(('seq', 'head')), may hold values from -8 to 8
- self_keys: bfloat16 [8192, 5120], P(('seq', 'head')), may hold values from -8 to 8
- self_values: bfloat16 [8192, 5120], P(('seq', 'head')), may hold values from -6 to 6
- text_queries: bfloat16 [8192, 5120], P(('seq', 'head')), may hold values from -8 to 8
- text_context: bfloat16 [32, 2, 512, 5120], P('seq', None, None, 'head'), may hold values from -8 to 8
- sample: int32 [32], replicated, may hold values from 0 to 31, each once
- text_lengths: int32 [32], replicated, may hold values from 128 to 512
- timestep: int32 [32], replicated, may hold values from 0 to 49
- time_gates: float32 [50, 5120], replicated, may hold values from 0.2 to 1.8
Outputs:
- self_attended: bfloat16 [8192, 5120], P(('seq', 'head'))
- cross_attended: bfloat16 [8192, 5120], P(('seq', 'head'))
The draws below stay inside these ranges and needn't reach their ends.
Inputs may be any that keep to these rules, and one draw needn't show every extreme that they name: Each index of a loaded sample appears once.
All inputs are finite; a program needn't handle non-finite values.
Results may differ from the reference program's by a relative error of at most 0.007.
Values may be sent and summed in bfloat16 or wider, within the bound.
No kernel may reach another device: no remote copies, remote signals or barrier semaphores. Data moves between devices by JAX's collectives and lax.ppermute only.
A program may use at most 192 MiB of HBM per device.

```python
import math
import jax
import jax.numpy as jnp
from jax import lax

HEADS = 40
HD = 128
D = 5120
TEXT = 512
STEPS = 50
TOKENS = 8192
SAMPLES = 32


def base_field(key, shape):
    return jnp.clip(1.6 * jax.random.normal(key, shape, jnp.float32), -8.0, 8.0)


def draw_self_queries(key, part):
    key = jax.random.fold_in(key, 1)
    field = base_field(key, (TOKENS, D))
    return field.astype(jnp.bfloat16)


def draw_self_keys(key, part):
    key = jax.random.fold_in(key, 2)
    field = base_field(key, (TOKENS, D))
    return field.astype(jnp.bfloat16)


def draw_text_queries(key, part):
    key = jax.random.fold_in(key, 3)
    field = base_field(key, (TOKENS, D))
    return field.astype(jnp.bfloat16)


def draw_text_context(key, part):
    key = jax.random.fold_in(key, 4)
    key_part, value_part = jax.random.split(key)
    key_field = base_field(key_part, (SAMPLES, TEXT, D))
    value_field = jnp.clip(jax.random.normal(value_part, (SAMPLES, TEXT, D), jnp.float32), -6.0, 6.0)
    return jnp.stack([key_field, value_field], axis=1).astype(jnp.bfloat16)


def plant(entries, rng, low, high):
    place = [jax.random.randint(jax.random.fold_in(rng, axis), (), 0, length) for axis, length in enumerate(entries.shape)]
    widest = entries.shape.index(max(entries.shape))
    next_to = place[:widest] + [(place[widest] + 1) % entries.shape[widest]] + place[widest + 1:]
    return entries.at[tuple(place)].set(low).at[tuple(next_to)].set(high)


def block_levels(rng, shape, cuts, low, high):
    level = 1.0
    for axis_at, blocks in cuts:
        steps = jax.random.uniform(jax.random.fold_in(jax.random.fold_in(rng, 6), axis_at), (blocks,), jnp.float32, low / len(cuts), high / len(cuts))
        level = level * jnp.repeat(jnp.exp(steps), shape[axis_at] // blocks).reshape((-1,) + (1,) * (len(shape) - 1 - axis_at))
    return level


def normal_values(key, extent, spread, limit, pieces=(), kind=jnp.bfloat16):
    drawn = spread * jax.random.normal(key, extent, jnp.float32)
    if pieces:
        drawn = drawn * block_levels(key, extent, pieces, -0.22, 0.18)
    return jnp.clip(drawn, -limit, limit).astype(kind)


def setup_inputs(seed: int = 0) -> dict:
    streams_of = jax.random.split(jax.random.key(seed), 10)
    self_queries = draw_self_queries(jax.random.fold_in(streams_of[9], 71), 0)
    self_keys = draw_self_keys(jax.random.fold_in(streams_of[9], 71), 0)
    self_values = normal_values(streams_of[2], (TOKENS, D), 1.0, 6.0, ((0, 256),))
    text_queries = draw_text_queries(jax.random.fold_in(streams_of[9], 71), 0)
    text_context = draw_text_context(jax.random.fold_in(streams_of[9], 71), 0)
    sample = jax.random.permutation(streams_of[5], SAMPLES).astype(jnp.int32)
    text_lengths = plant(jax.random.randint(streams_of[6], (SAMPLES,), max(8, TEXT // 4), TEXT + 1), jax.random.fold_in(streams_of[6], 1), max(8, TEXT // 4), TEXT).astype(jnp.int32)
    timestep = plant(jax.random.randint(streams_of[7], (SAMPLES,), 0, STEPS), jax.random.fold_in(streams_of[7], 1), 0, STEPS - 1).astype(jnp.int32)
    time_gates = jnp.clip(jax.random.uniform(streams_of[8], (STEPS, D), jnp.float32, 0.2, 1.8), 0.2, 1.8)
    return {"self_queries": self_queries, "self_keys": self_keys, "self_values": self_values, "text_queries": text_queries, "text_context": text_context, "sample": sample, "text_lengths": text_lengths, "timestep": timestep, "time_gates": time_gates}


def softmax_rows(scores, value_rows):
    maxima = lax.optimization_barrier(jnp.max(scores, axis=-1, keepdims=True))
    weights = jnp.exp(scores - maxima)
    totals = lax.optimization_barrier(jnp.sum(weights, axis=-1, keepdims=True))
    summed = jnp.dot(weights.astype(jnp.bfloat16), value_rows, preferred_element_type=jnp.float32)
    return (summed / totals).astype(jnp.bfloat16)

def split_heads(matrix):
    return matrix.reshape(matrix.shape[0], HEADS, HD).transpose(1, 0, 2)

def join_heads(stacked):
    return stacked.transpose(1, 0, 2).reshape(stacked.shape[1], HEADS * HD)

def reference(self_queries, self_keys, self_values, text_queries, text_context, sample, text_lengths, timestep, time_gates):
    factor = 1.0 / math.sqrt(HD)
    chosen = sample[0]

    def self_head(operands):
        query_rows, key_rows, value_rows = operands
        scores = jnp.dot(query_rows, key_rows.T, preferred_element_type=jnp.float32) * factor
        return softmax_rows(scores, value_rows)
    attended = join_heads(lax.map(self_head, (split_heads(self_queries), split_heads(self_keys), split_heads(self_values))))
    step_index = lax.dynamic_index_in_dim(timestep, chosen, 0, keepdims=False)
    gate_row = lax.dynamic_index_in_dim(time_gates, step_index, 0, keepdims=False)
    self_attended = (gate_row[None, :] * attended.astype(jnp.float32)).astype(jnp.bfloat16)
    context = lax.dynamic_index_in_dim(text_context, chosen, 0, keepdims=False)
    length = lax.dynamic_index_in_dim(text_lengths, chosen, 0, keepdims=False)
    valid_keys = jnp.arange(TEXT) < length

    def cross_head(operands):
        query_rows, key_rows, value_rows = operands
        scores = jnp.dot(query_rows, key_rows.T, preferred_element_type=jnp.float32) * factor
        scores = jnp.where(valid_keys[None, :], scores, jnp.float32(-1e+30))
        return softmax_rows(scores, value_rows)
    cross_attended = join_heads(lax.map(cross_head, (split_heads(text_queries), split_heads(context[0]), split_heads(context[1]))))
    return (self_attended, cross_attended)
```

```python
import functools
import math

import jax
import jax.numpy as jnp
from jax import lax
from jax.experimental import pallas as pl
from jax.experimental.pallas import tpu as pltpu
from jax.sharding import Mesh, PartitionSpec as P

AXES = ("z", "xl", "core", "xh", "y")
SIZES = (8, 2, 2, 2, 4)
PLANE = ("xl", "core", "xh", "y")

HD = 128
ROWS = 32
GROUPS = 8
SPLIT = 4
PEERS = GROUPS * SPLIT
PLANE_ROWS = PEERS * ROWS
TEXT = 512
SCALE = math.log2(math.e) / math.sqrt(HD)
F32 = jnp.float32
BF16 = jnp.bfloat16
VMEM_LIMIT = 48 * 1024 * 1024


def call(kernel, out_shape, cost=None, **kwargs):
    return pl.pallas_call(
        kernel,
        out_shape=out_shape,
        cost_estimate=cost,
        compiler_params=pltpu.CompilerParams(vmem_limit_bytes=VMEM_LIMIT),
        **kwargs,
    )


def head_columns(head):
    return slice(head * HD, (head + 1) * HD)


def pack_pairs_kernel(keys_ref, values_ref, out_ref):
    quarter = ROWS // SPLIT
    for j in range(GROUPS):
        fifth = head_columns(5 * j + 4)
        key_rows = keys_ref[:, fifth].astype(F32)
        value_rows = values_ref[:, fifth].astype(F32)
        for i in range(SPLIT):
            to = i * GROUPS + j
            own = head_columns(5 * j + i)
            out_ref[to, 0:32, :] = keys_ref[:, own]
            out_ref[to, 32:64, :] = values_ref[:, own]
            part = slice(i * quarter, (i + 1) * quarter)
            out_ref[to, 64:80, :] = jnp.concatenate([key_rows[part], value_rows[part]]).astype(BF16)


def pack_queries_kernel(queries_ref, text_queries_ref, out_ref):
    for j in range(GROUPS):
        for i in range(SPLIT):
            to = i * GROUPS + j
            own, fifth = head_columns(5 * j + i), head_columns(5 * j + 4)
            out_ref[to, 0:32, :] = queries_ref[:, own]
            out_ref[to, 32:64, :] = queries_ref[:, fifth]
            out_ref[to, 64:96, :] = text_queries_ref[:, own]
            out_ref[to, 96:128, :] = text_queries_ref[:, fifth]


def pack_text_kernel(core_ref, text_ref, keep_ref, send_ref):
    quarter = TEXT // SPLIT

    def write(ref, core):
        for xl in range(2):
            i = xl * 2 + core
            for kind in range(2):
                base = kind * (TEXT + quarter)
                ref[xl, base : base + TEXT, :] = text_ref[0, kind, :, head_columns(i)]
                ref[xl, base + TEXT : base + TEXT + quarter, :] = text_ref[
                    0, kind, i * quarter : (i + 1) * quarter, head_columns(4)
                ]

    @pl.when(core_ref[0] == 0)
    def _():
        write(keep_ref, 0)
        write(send_ref, 1)

    @pl.when(core_ref[0] != 0)
    def _():
        write(keep_ref, 1)
        write(send_ref, 0)


def scores_of(queries, keys):
    return lax.dot_general(queries, keys, (((1,), (1,)), ((), ())), preferred_element_type=F32)


def attend(queries, keys, values, state):
    scores = jnp.concatenate([scores_of(queries, k) for k in keys], axis=1) if len(keys) > 1 else scores_of(queries, keys[0])
    return fold(scores, values, state)


def fold(scores, values, state):
    top = jnp.max(scores, axis=1, keepdims=True)
    if state is not None:
        top = jnp.maximum(top, state[0])
    weights = jnp.exp2((scores - top) * SCALE)
    total = jnp.sum(weights, axis=1, keepdims=True)
    weights = weights.astype(BF16)
    summed, at = None, 0
    for v in values:
        term = jnp.dot(weights[:, at : at + v.shape[0]], v, preferred_element_type=F32)
        summed = term if summed is None else summed + term
        at += v.shape[0]
    if state is not None:
        shrink = jnp.exp2((state[0] - top) * SCALE)
        total = total + state[1] * shrink
        summed = summed + state[2] * shrink
    return top, total, summed


def write_result(out_ref, whole, part):
    count = out_ref.shape[0]
    out_ref[:, 0:32, :] = (whole[2] / whole[1]).astype(BF16).reshape(count, ROWS, HD)
    out_ref[:, 32:64, :] = (part[2] / part[1]).astype(BF16).reshape(count, ROWS, HD)
    size = part[0] * SCALE + jnp.log2(part[1])
    size = jnp.broadcast_to(size, (count * ROWS, HD))
    high = size.astype(BF16).astype(F32)
    middle = (size - high).astype(BF16).astype(F32)
    low = size - high - middle
    lane = lax.broadcasted_iota(jnp.int32, (count * ROWS, HD), 1)
    row = lax.broadcasted_iota(jnp.int32, (count * ROWS, HD), 0)
    terms = jnp.where(lane < 32, high, jnp.where(lane < 64, middle, low))
    terms = jnp.where((lane % 32 == row % 32) & (lane < 96), terms, 0.0)
    terms = jnp.sum(terms.reshape(count, ROWS, HD), axis=1, keepdims=True)
    out_ref[:, 64:80, :] = jnp.broadcast_to(terms, (count, 16, HD)).astype(BF16)


def self_kernel(shards, first, last, *refs):
    queries_ref, shard_refs, rest = refs[0], refs[1 : 1 + shards], refs[1 + shards :]
    if not first:
        whole_ref, part_ref, stats_ref = rest[:3]
        rest = rest[3:]
    block = queries_ref.shape[0] * ROWS
    keys, values, part_keys, part_values = [], [], [], []
    for ref in shard_refs:
        count = ref.shape[0]
        keys.append(ref[:, 0:32, :].reshape(count * 32, HD))
        values.append(ref[:, 32:64, :].reshape(count * 32, HD))
        quarter = ref[:, 64:80, :].astype(F32)
        part_keys.append(quarter[:, 0:8].reshape(count * 8, HD).astype(BF16))
        part_values.append(quarter[:, 8:16].reshape(count * 8, HD).astype(BF16))
    whole_state = part_state = None
    if not first:
        stats = stats_ref[...]
        whole_state = (stats[:, 0:1], stats[:, 1:2], whole_ref[...])
        part_state = (stats[:, 2:3], stats[:, 3:4], part_ref[...])
    whole = attend(queries_ref[:, 0:32, :].reshape(block, HD), keys, values, whole_state)
    part = attend(queries_ref[:, 32:64, :].reshape(block, HD), part_keys, part_values, part_state)
    if last:
        write_result(rest[0], whole, part)
        return
    whole_out, part_out, stats_out = rest
    whole_out[...] = whole[2]
    part_out[...] = part[2]
    lane = lax.broadcasted_iota(jnp.int32, (block, HD), 1)
    stats_out[...] = jnp.where(
        lane == 0, whole[0], jnp.where(lane == 1, whole[1], jnp.where(lane == 2, part[0], part[1]))
    )


def self_step(queries, shards, state, last=False):
    first = state is None
    senders = 8
    block = senders * ROWS
    steps = PEERS // senders
    state_specs = [pl.BlockSpec((block, HD), lambda g: (g, 0))] * 3
    in_specs = [pl.BlockSpec((senders, 128, HD), lambda g: (g, 0, 0))]
    in_specs += [pl.BlockSpec(s.shape, lambda g: (0, 0, 0)) for s in shards]
    in_specs += [] if first else state_specs
    if last:
        out_shape = jax.ShapeDtypeStruct((PEERS, 80, HD), BF16)
        out_specs = pl.BlockSpec((senders, 80, HD), lambda g: (g, 0, 0))
    else:
        out_shape = [jax.ShapeDtypeStruct((PLANE_ROWS, HD), F32)] * 3
        out_specs = state_specs
    keys = sum(s.shape[0] for s in shards) * 40
    cost = pl.CostEstimate(
        flops=4 * PLANE_ROWS * keys * HD * 2,
        bytes_accessed=keys * HD * 4 + PLANE_ROWS * HD * 16,
        transcendentals=PLANE_ROWS * keys,
    )
    return call(
        functools.partial(self_kernel, len(shards), first, last),
        out_shape,
        cost,
        grid=(steps,),
        in_specs=in_specs,
        out_specs=out_specs,
    )(queries, *shards, *(() if first else state))


def cross_kernel(scalars_ref, queries_ref, text_ref, out_ref):
    length, place = scalars_ref[0], scalars_ref[1]
    quarter = TEXT // SPLIT
    block = queries_ref.shape[0] * ROWS

    def masked(scores, start):
        at = start + lax.broadcasted_iota(jnp.int32, scores.shape, 1)
        return jnp.where(at < length, scores, -1e30)

    whole = fold(
        masked(scores_of(queries_ref[:, 64:96, :].reshape(block, HD), text_ref[0:512, :]), 0),
        [text_ref[640:1152, :]],
        None,
    )
    part = fold(
        masked(scores_of(queries_ref[:, 96:128, :].reshape(block, HD), text_ref[512:640, :]), place * quarter),
        [text_ref[1152:1280, :]],
        None,
    )
    write_result(out_ref, whole, part)


def cross_step(scalars, queries, text):
    senders = 8
    return call(
        cross_kernel,
        jax.ShapeDtypeStruct((PEERS, 80, HD), BF16),
        pl.CostEstimate(
            flops=4 * PLANE_ROWS * 640 * HD * 2, bytes_accessed=2 * 1024 * 1024, transcendentals=PLANE_ROWS * 640
        ),
        grid=(PEERS // senders,),
        in_specs=[
            pl.BlockSpec(memory_space=pltpu.SMEM),
            pl.BlockSpec((senders, 128, HD), lambda g: (g, 0, 0)),
            pl.BlockSpec(text.shape, lambda g: (0, 0)),
        ],
        out_specs=pl.BlockSpec((senders, 80, HD), lambda g: (g, 0, 0)),
    )(scalars, queries, text)


def merged(message_ref, j):
    lane = lax.broadcasted_iota(jnp.int32, (ROWS, HD), 1)
    row = lax.broadcasted_iota(jnp.int32, (ROWS, HD), 0)
    mine = (lane % 32 == row) & (lane < 96)
    sizes = []
    for i in range(SPLIT):
        terms = message_ref[i * GROUPS + j, 64:80, :].astype(F32)[0:1]
        sizes.append(jnp.sum(jnp.where(mine, jnp.broadcast_to(terms, (ROWS, HD)), 0.0), axis=1, keepdims=True))
    top = functools.reduce(jnp.maximum, sizes)
    shares = [jnp.exp2(s - top) for s in sizes]
    summed = sum(
        share * message_ref[i * GROUPS + j, 32:64, :].astype(F32) for i, share in enumerate(shares)
    )
    return (summed / sum(shares)).astype(BF16)


def unpack_kernel(gated, *refs):
    message_ref, out_ref = refs[0], refs[-1]
    for j in range(GROUPS):
        for i in range(SPLIT + 1):
            columns = head_columns(5 * j + i)
            rows = message_ref[i * GROUPS + j, 0:32, :] if i < SPLIT else merged(message_ref, j)
            if gated:
                rows = (refs[1][0:1, columns] * rows.astype(F32)).astype(BF16)
            out_ref[:, columns] = rows


def unpack(message, gate=None):
    operands = [message] if gate is None else [message, gate]
    return call(
        functools.partial(unpack_kernel, gate is not None), jax.ShapeDtypeStruct((ROWS, 40 * HD), BF16)
    )(*operands)


def exchange(messages):
    return lax.all_to_all(messages, PLANE, split_axis=0, concat_axis=0, tiled=True)


def shift(block, by):
    size = SIZES[0]
    return lax.ppermute(block, "z", [(z, (z + by) % size) for z in range(size)])


def pick(block, index):
    return lax.dynamic_index_in_dim(block, index, 0, keepdims=False)


def text_of_sample(text_context, chosen):
    z, xl, core = lax.axis_index("z"), lax.axis_index("xl"), lax.axis_index("core")
    part = jax.ShapeDtypeStruct((2, 1280, HD), BF16)
    keep, send = call(
        pack_text_kernel,
        [part, part],
        in_specs=[pl.BlockSpec(memory_space=pltpu.SMEM), pl.BlockSpec(memory_space=pltpu.VMEM)],
    )(core.reshape(1), text_context)
    got = lax.ppermute(send, "core", [(0, 1), (1, 0)])
    held = jnp.where(chosen % 2 == core, keep, got)
    got = lax.ppermute(pick(held, 1 - xl), "xl", [(0, 1), (1, 0)])
    held = jnp.where(chosen // 2 % 2 == xl, pick(held, xl), got)
    pieces = lax.all_to_all(held.reshape(8, 160, HD), "z", split_axis=0, concat_axis=0, tiled=True)
    piece = pick(pieces, chosen // 4)
    return lax.all_gather(piece, "z", axis=0, tiled=True)


def on_device(
    self_queries,
    self_keys,
    self_values,
    text_queries,
    text_context,
    sample,
    text_lengths,
    timestep,
    time_gates,
):
    chosen = sample[0]
    pairs = call(pack_pairs_kernel, jax.ShapeDtypeStruct((PEERS, 80, HD), BF16))(self_keys, self_values)
    pairs = exchange(pairs)
    queries = call(pack_queries_kernel, jax.ShapeDtypeStruct((PEERS, 128, HD), BF16))(self_queries, text_queries)
    queries, pairs = lax.optimization_barrier((queries, pairs))
    queries = exchange(queries)

    half = PEERS // 2
    own = [pairs[:half], pairs[half:]]
    up = [shift(b, 1) for b in own]
    down = [shift(b, -1) for b in own]
    state = self_step(queries, own, None)
    for _ in range(2):
        up_next = [shift(b, 1) for b in up]
        down_next = [shift(b, -1) for b in down]
        state = self_step(queries, up + down, state)
        up, down = up_next, down_next
    far = [shift(up[0], 1), shift(down[1], -1)]
    state = self_step(queries, up + down, state)
    result = exchange(self_step(queries, far, state, last=True))

    text = text_of_sample(text_context, chosen)
    length = pick(text_lengths, chosen)
    place = lax.axis_index("xl") * 2 + lax.axis_index("core")
    cross = exchange(cross_step(jnp.stack([length, place]), queries, text))
    gate = lax.dynamic_slice_in_dim(time_gates, pick(timestep, chosen), 1, 0)
    return (unpack(result, gate), unpack(cross))


def solution(mesh):
    fine = Mesh(mesh.devices.reshape(SIZES), AXES)
    rows = P(AXES, None)
    in_specs = (rows, rows, rows, rows, P(("z", "xl", "core"), None, None, ("xh", "y")), P(), P(), P(), P())
    return jax.shard_map(on_device, mesh=fine, in_specs=in_specs, out_specs=(rows, rows), check_vma=False)
```

```python
import functools
import math

import jax
import jax.numpy as jnp
from jax import lax
from jax.experimental import pallas as pl
from jax.experimental.pallas import tpu as pltpu
from jax.sharding import Mesh, PartitionSpec as P

AXES = ("z", "xl", "core", "xh", "y")
SIZES = (8, 2, 2, 2, 4)
PLANES = SIZES[0]
PLANE = ("xl", "core", "xh", "y")
COLUMN = ("z", "y")
RING = ("xl", "xh")
RING_ORDER = (0, 2, 1, 3)

HD = 128
ROWS = 32
GROUPS = 8
SPLIT = 4
PEERS = GROUPS * SPLIT
PLANE_ROWS = PEERS * ROWS
TEXT = 512
SCALE = math.log2(math.e) / math.sqrt(HD)
F32 = jnp.float32
BF16 = jnp.bfloat16
VMEM_LIMIT = 62 * 1024 * 1024


def whole_block(shape):
    return pl.BlockSpec(shape, lambda step: (0,) * len(shape))


def call(kernel, out_shape, operands, cost=None, scalars=0, specs=()):
    in_specs = [pl.BlockSpec(memory_space=pltpu.SMEM)] * scalars + list(specs)
    in_specs += [whole_block(x.shape) for x in operands[len(in_specs) :]]
    return pl.pallas_call(
        kernel,
        out_shape=out_shape,
        grid=(1,),
        in_specs=in_specs,
        out_specs=jax.tree.map(lambda x: whole_block(x.shape), out_shape),
        cost_estimate=cost,
        compiler_params=pltpu.CompilerParams(vmem_limit_bytes=VMEM_LIMIT),
    )(*operands)


def query_rows():
    return pl.BlockSpec((PEERS, 64, HD), lambda step: (0, 0, 0))


def head_columns(head):
    return slice(head * HD, (head + 1) * HD)


def self_slot(i, j):
    return j * SPLIT + i


def cross_slot(i, j):
    return i * GROUPS + j


def pack_kernel(keys_ref, values_ref, queries_ref, out_ref):
    quarter = ROWS // SPLIT
    for j in range(GROUPS):
        fifth = head_columns(5 * j + 4)
        key_rows = keys_ref[:, fifth].astype(F32)
        value_rows = values_ref[:, fifth].astype(F32)
        for i in range(SPLIT):
            to = self_slot(i, j)
            own = head_columns(5 * j + i)
            out_ref[to, 0:32, :] = queries_ref[:, own]
            out_ref[to, 32:64, :] = queries_ref[:, fifth]
            out_ref[to, 64:96, :] = keys_ref[:, own]
            out_ref[to, 96:128, :] = values_ref[:, own]
            part = slice(i * quarter, (i + 1) * quarter)
            out_ref[to, 128:144, :] = jnp.concatenate([key_rows[part], value_rows[part]]).astype(BF16)


def pack_queries_kernel(queries_ref, out_ref):
    for j in range(GROUPS):
        for i in range(SPLIT):
            to = cross_slot(i, j)
            out_ref[to, 0:32, :] = queries_ref[:, head_columns(5 * j + i)]
            out_ref[to, 32:64, :] = queries_ref[:, head_columns(5 * j + 4)]


def pack_text_kernel(core_ref, text_ref, keep_ref, send_ref):
    quarter = TEXT // SPLIT

    def write(ref, core):
        for xl in range(2):
            i = xl * 2 + core
            for kind in range(2):
                base = kind * (TEXT + quarter)
                ref[xl, base : base + TEXT, :] = text_ref[0, kind, :, head_columns(i)]
                ref[xl, base + TEXT : base + TEXT + quarter, :] = text_ref[
                    0, kind, i * quarter : (i + 1) * quarter, head_columns(4)
                ]

    @pl.when(core_ref[0] == 0)
    def _():
        write(keep_ref, 0)
        write(send_ref, 1)

    @pl.when(core_ref[0] != 0)
    def _():
        write(keep_ref, 1)
        write(send_ref, 0)


def scaled_queries(queries):
    scaled = queries.astype(F32) * SCALE
    high = scaled.astype(BF16)
    low = (scaled - high.astype(F32)).astype(BF16)
    return jnp.concatenate([high, low], axis=1)


def products(queries, keys):
    return lax.dot_general(queries, keys, (((1,), (1,)), ((), ())), preferred_element_type=F32)


def twice(keys):
    return jnp.concatenate([keys, keys], axis=1)


def with_ones(values):
    return jnp.concatenate([values, jnp.ones_like(values)], axis=1)


def fold(scores, values, state):
    top = jnp.max(scores, axis=1, keepdims=True)
    if state is not None:
        top = jnp.maximum(top, state[0])
    weights = jnp.exp2(scores - top).astype(BF16)
    summed = jnp.dot(weights, values, preferred_element_type=F32)
    total, summed = summed[:, HD : HD + 1], summed[:, :HD]
    if state is not None:
        shrink = jnp.exp2(state[0] - top)
        total = total + state[1] * shrink
        summed = summed + state[2] * shrink
    return top, total, summed


def write_result(out_ref, to, whole, part):
    count = to.size
    out_ref[to, 0:32, :] = (whole[2] / whole[1]).astype(BF16).reshape(count, ROWS, HD)
    out_ref[to, 32:64, :] = (part[2] / part[1]).astype(BF16).reshape(count, ROWS, HD)
    size = part[0] + jnp.log2(part[1])
    size = jnp.broadcast_to(size, (count * ROWS, HD))
    high = size.astype(BF16).astype(F32)
    middle = (size - high).astype(BF16).astype(F32)
    low = size - high - middle
    lane = lax.broadcasted_iota(jnp.int32, (count * ROWS, HD), 1)
    row = lax.broadcasted_iota(jnp.int32, (count * ROWS, HD), 0)
    terms = jnp.where(lane < 32, high, jnp.where(lane < 64, middle, low))
    terms = jnp.where((lane % 32 == row % 32) & (lane < 96), terms, 0.0)
    terms = jnp.sum(terms.reshape(count, ROWS, HD), axis=1, keepdims=True)
    out_ref[to, 64:80, :] = jnp.broadcast_to(terms, (count, 16, HD)).astype(BF16)


def fold_lazily(scaled, keys, values, state):
    top, total, summed = state
    excess = None
    for at in range(0, keys.shape[0], CHUNK):
        part = slice(at, min(at + CHUNK, keys.shape[0]))
        scores = products(scaled, keys[part]) - top
        most = jnp.max(scores.reshape(-1, 8, scores.shape[1]), axis=0)
        most = functools.reduce(jnp.maximum, [most[:, t : t + HD] for t in range(0, most.shape[1], HD)])
        excess = most if excess is None else jnp.maximum(excess, most)
        term = jnp.dot(jnp.exp2(scores).astype(BF16), values[part], preferred_element_type=F32)
        total = total + term[:, HD : HD + 1]
        summed = summed + term[:, :HD]
    return (top, total, summed), excess


SENDERS = 8
CHUNK = 512
MOST = 64.0


def keys_and_values(shard_refs):
    keys, values, part_keys, part_values = [], [], [], []
    for ref in shard_refs:
        count = ref.shape[0]
        keys.append(ref[:, 0:32, :].reshape(count * 32, HD))
        values.append(ref[:, 32:64, :].reshape(count * 32, HD))
        quarter = ref[:, 64:80, :].astype(F32)
        part_keys.append(quarter[:, 0:8].reshape(count * 8, HD).astype(BF16))
        part_values.append(quarter[:, 8:16].reshape(count * 8, HD).astype(BF16))
    return (
        (twice(jnp.concatenate(keys)), with_ones(jnp.concatenate(values))),
        (twice(jnp.concatenate(part_keys)), with_ones(jnp.concatenate(part_values))),
    )


def self_kernel(shards, first, last, *refs):
    queries_ref, shard_refs, rest = refs[0], refs[1 : 1 + shards], refs[1 + shards :]
    if not first:
        whole_ref, part_ref, stats_ref = rest[:3]
        rest = rest[3:]
    block = SENDERS * ROWS

    def queries_of(senders):
        return [scaled_queries(queries_ref[senders, at : at + 32, :].reshape(block, HD)) for at in (0, 32)]

    def states_of(rows):
        stats = stats_ref[rows]
        return (stats[:, 0:1], stats[:, 1:2], whole_ref[rows]), (stats[:, 2:3], stats[:, 3:4], part_ref[rows])

    def write(senders, rows, whole, part):
        if last:
            write_result(rest[0], senders, whole, part)
            return
        whole_out, part_out, stats_out = rest
        whole_out[rows] = whole[2]
        part_out[rows] = part[2]
        lane = lax.broadcasted_iota(jnp.int32, (block, HD), 1)
        stats_out[rows] = jnp.where(
            lane == 0, whole[0], jnp.where(lane == 1, whole[1], jnp.where(lane == 2, part[0], part[1]))
        )

    def places(index):
        start = index * block if isinstance(index, int) else pl.multiple_of(index * block, block)
        return pl.ds(index * SENDERS, SENDERS), pl.ds(start, block)

    pairs = keys_and_values(shard_refs)
    excess = None
    for index in range(PEERS // SENDERS):
        senders, rows = places(index)
        scaled = queries_of(senders)
        if first:
            write(senders, rows, *(fold(products(q, k), v, None) for q, (k, v) in zip(scaled, pairs)))
            continue
        done = [fold_lazily(q, k, v, state) for q, (k, v), state in zip(scaled, pairs, states_of(rows))]
        write(senders, rows, done[0][0], done[1][0])
        for _, most in done:
            excess = most if excess is None else jnp.maximum(excess, most)
    if first:
        return

    @pl.when(jnp.max(excess) > MOST)
    def _():
        again = keys_and_values(shard_refs)

        def redo(index, carry):
            senders, rows = places(index)
            found = [
                fold(products(q, k), v, state)
                for q, (k, v), state in zip(queries_of(senders), again, states_of(rows))
            ]
            write(senders, rows, *found)
            return carry

        lax.fori_loop(0, PEERS // SENDERS, redo, 0)


def self_step(queries, shards, state, last=False):
    first = state is None
    if last:
        out_shape = jax.ShapeDtypeStruct((PEERS, 80, HD), BF16)
    else:
        out_shape = [jax.ShapeDtypeStruct((PLANE_ROWS, HD), F32)] * 3
    keys = sum(s.shape[0] for s in shards) * 40
    cost = pl.CostEstimate(
        flops=4 * PLANE_ROWS * keys * HD * 2,
        bytes_accessed=keys * HD * 4 + PLANE_ROWS * HD * 16,
        transcendentals=PLANE_ROWS * keys,
    )
    operands = (queries, *shards, *(() if first else state))
    kernel = functools.partial(self_kernel, len(shards), first, last)
    return call(kernel, out_shape, operands, cost, specs=[query_rows()])


def cross_kernel(scalars_ref, queries_ref, text_ref, out_ref):
    length, place = scalars_ref[0], scalars_ref[1]
    quarter = TEXT // SPLIT
    block = SENDERS * ROWS

    def masked(scores, start):
        at = start + lax.broadcasted_iota(jnp.int32, scores.shape, 1)
        return jnp.where(at < length, scores, -1e30)

    keys, part_keys = twice(text_ref[0:512, :]), twice(text_ref[512:640, :])
    values, part_values = with_ones(text_ref[640:1152, :]), with_ones(text_ref[1152:1280, :])
    for index in range(PEERS // SENDERS):
        senders = pl.ds(index * SENDERS, SENDERS)
        scaled = [scaled_queries(queries_ref[senders, at : at + 32, :].reshape(block, HD)) for at in (0, 32)]
        whole = fold(masked(products(scaled[0], keys), 0), values, None)
        part = fold(masked(products(scaled[1], part_keys), place * quarter), part_values, None)
        write_result(out_ref, senders, whole, part)


def cross_step(scalars, queries, text):
    cost = pl.CostEstimate(
        flops=4 * PLANE_ROWS * 640 * HD * 2, bytes_accessed=2 * 1024 * 1024, transcendentals=PLANE_ROWS * 640
    )
    out_shape = jax.ShapeDtypeStruct((PEERS, 80, HD), BF16)
    return call(cross_kernel, out_shape, (scalars, queries, text), cost, scalars=1, specs=[query_rows()])


def merged(message_ref, slot, j):
    lane = lax.broadcasted_iota(jnp.int32, (ROWS, HD), 1)
    row = lax.broadcasted_iota(jnp.int32, (ROWS, HD), 0)
    mine = (lane % 32 == row) & (lane < 96)
    sizes = []
    for i in range(SPLIT):
        terms = message_ref[slot(i, j), 64:80, :].astype(F32)[0:1]
        sizes.append(jnp.sum(jnp.where(mine, jnp.broadcast_to(terms, (ROWS, HD)), 0.0), axis=1, keepdims=True))
    top = functools.reduce(jnp.maximum, sizes)
    shares = [jnp.exp2(s - top) for s in sizes]
    summed = sum(
        share * message_ref[slot(i, j), 32:64, :].astype(F32) for i, share in enumerate(shares)
    )
    return (summed / sum(shares)).astype(BF16)


def unpack_kernel(slot, gated, *refs):
    message_ref, out_ref = refs[0], refs[-1]
    for j in range(GROUPS):
        for i in range(SPLIT + 1):
            columns = head_columns(5 * j + i)
            rows = message_ref[slot(i, j), 0:32, :] if i < SPLIT else merged(message_ref, slot, j)
            if gated:
                rows = (refs[1][0:1, columns] * rows.astype(F32)).astype(BF16)
            out_ref[:, columns] = rows


def unpack(slot, message, gate=None):
    operands = [message] if gate is None else [message, gate]
    out_shape = jax.ShapeDtypeStruct((ROWS, 40 * HD), BF16)
    return call(functools.partial(unpack_kernel, slot, gate is not None), out_shape, operands)


def exchange(messages, group):
    return lax.all_to_all(messages, group, split_axis=0, concat_axis=0, tiled=True)


def shift(block, by):
    pairs = [(RING_ORDER[x], RING_ORDER[(x + by) % 4]) for x in range(4)]
    return lax.ppermute(block, RING, pairs)


def swap(block, axis, distance=1):
    size = dict(zip(AXES, SIZES))[axis]
    return lax.ppermute(block, axis, [(at, at ^ distance) for at in range(size)])


def pick(block, index):
    return lax.dynamic_index_in_dim(block, index, 0, keepdims=False)


def text_of_plane(text_context, chosen):
    xl, core = lax.axis_index("xl"), lax.axis_index("core")
    part = jax.ShapeDtypeStruct((2, 1280, HD), BF16)
    keep, send = call(pack_text_kernel, [part, part], (core.reshape(1), text_context), scalars=1)
    held = jnp.where(chosen % 2 == core, keep, swap(send, "core"))
    return jnp.where(chosen // 2 % 2 == xl, pick(held, xl), swap(pick(held, 1 - xl), "xl"))


def text_along_z(held, distance, chosen):
    agrees = (lax.axis_index("z") ^ (chosen // 4)) & distance == 0
    return jnp.where(agrees, held, swap(held, "z", distance))


def on_device(
    self_queries,
    self_keys,
    self_values,
    text_queries,
    text_context,
    sample,
    text_lengths,
    timestep,
    time_gates,
):
    chosen = sample[0]
    barrier = lax.optimization_barrier
    def message(rows):
        return jax.ShapeDtypeStruct((PEERS, rows, HD), BF16)

    blocks = call(pack_kernel, message(144), (self_keys, self_values, self_queries))
    text_blocks = call(pack_queries_kernel, message(64), (text_queries,))
    text = text_of_plane(text_context, chosen)
    queries = exchange(blocks, COLUMN)
    queries, text_blocks, text = barrier((queries, text_blocks, text))
    own = queries[:, 64:144]
    half = PEERS // 2

    up, down, other = shift(own, 1), shift(own, -1), swap(own, "core")
    text = text_along_z(text, 4, chosen)
    state = self_step(queries, [own], None)
    cross_queries = exchange(text_blocks, PLANE)
    up, down, other, text, state = barrier((up, down, other, text, state))

    far = [shift(up[:half], 1), shift(down[half:], -1)]
    other_up, other_down = swap(up, "core"), swap(down, "core")
    text = text_along_z(text, 2, chosen)
    state = self_step(queries, [other, up, down], state)
    far, other_up, other_down, text, state, cross_queries = barrier(
        (far, other_up, other_down, text, state, cross_queries)
    )

    other_far = [swap(x, "core") for x in far]
    text = text_along_z(text, 1, chosen)
    state = self_step(queries, [other_up, other_down, *far], state)
    other_far, text, state = barrier((other_far, text, state))

    place = lax.axis_index("xl") * 2 + lax.axis_index("core")
    cross = cross_step(jnp.stack([pick(text_lengths, chosen), place]), cross_queries, text)
    cross = exchange(cross, PLANE)
    result = exchange(self_step(queries, other_far, state, last=True), COLUMN)
    gate = lax.dynamic_slice_in_dim(time_gates, pick(timestep, chosen), 1, 0)
    return (unpack(self_slot, result, gate), unpack(cross_slot, cross))


def solution(mesh):
    fine = Mesh(mesh.devices.reshape(SIZES), AXES)
    rows = P(AXES, None)
    in_specs = (rows, rows, rows, rows, P(AXES[:3], None, None, AXES[3:]), P(), P(), P(), P())
    return jax.shard_map(on_device, mesh=fine, in_specs=in_specs, out_specs=(rows, rows), check_vma=False)
```

```python
import functools
import math

import jax
import jax.numpy as jnp
from jax import lax
from jax.experimental import pallas as pl
from jax.experimental.pallas import tpu as pltpu
from jax.sharding import Mesh, PartitionSpec as P

AXES = ("z", "xl", "core", "xh", "y")
SIZES = (8, 2, 2, 2, 4)
PLANES = SIZES[0]
PLANE = ("xl", "core", "xh", "y")
COLUMN = ("z", "y")
RING = ("xl", "xh")
RING_ORDER = (0, 2, 1, 3)

HD = 128
ROWS = 32
GROUPS = 8
SPLIT = 4
PEERS = GROUPS * SPLIT
PLANE_ROWS = PEERS * ROWS
TEXT = 512
SCALE = math.log2(math.e) / math.sqrt(HD)
F32 = jnp.float32
BF16 = jnp.bfloat16
VMEM_LIMIT = 63 * 1024 * 1024


def whole_block(shape):
    return pl.BlockSpec(shape, lambda step: (0,) * len(shape))


def call(kernel, out_shape, operands, cost=None, scalars=0, specs=()):
    in_specs = [pl.BlockSpec(memory_space=pltpu.SMEM)] * scalars + list(specs)
    in_specs += [whole_block(x.shape) for x in operands[len(in_specs) :]]
    return pl.pallas_call(
        kernel,
        out_shape=out_shape,
        grid=(1,),
        in_specs=in_specs,
        out_specs=jax.tree.map(lambda x: whole_block(x.shape), out_shape),
        cost_estimate=cost,
        compiler_params=pltpu.CompilerParams(vmem_limit_bytes=VMEM_LIMIT),
    )(*operands)


def query_rows():
    return pl.BlockSpec((PEERS, 64, HD), lambda step: (0, 0, 0))


def head_columns(head):
    return slice(head * HD, (head + 1) * HD)


def self_slot(i, j):
    return j * SPLIT + i


def cross_slot(i, j):
    return i * GROUPS + j


def pack_kernel(keys_ref, values_ref, queries_ref, out_ref):
    quarter = ROWS // SPLIT
    for j in range(GROUPS):
        fifth = head_columns(5 * j + 4)
        key_rows = keys_ref[:, fifth].astype(F32)
        value_rows = values_ref[:, fifth].astype(F32)
        for i in range(SPLIT):
            to = self_slot(i, j)
            own = head_columns(5 * j + i)
            out_ref[to, 0:32, :] = queries_ref[:, own]
            out_ref[to, 32:64, :] = queries_ref[:, fifth]
            out_ref[to, 64:96, :] = keys_ref[:, own]
            out_ref[to, 96:128, :] = values_ref[:, own]
            part = slice(i * quarter, (i + 1) * quarter)
            out_ref[to, 128:144, :] = jnp.concatenate([key_rows[part], value_rows[part]]).astype(BF16)


def pack_queries_kernel(queries_ref, out_ref):
    for j in range(GROUPS):
        for i in range(SPLIT):
            to = cross_slot(i, j)
            out_ref[to, 0:32, :] = queries_ref[:, head_columns(5 * j + i)]
            out_ref[to, 32:64, :] = queries_ref[:, head_columns(5 * j + 4)]


def pack_text_kernel(core_ref, text_ref, keep_ref, send_ref):
    quarter = TEXT // SPLIT

    def write(ref, core):
        for xl in range(2):
            i = xl * 2 + core
            for kind in range(2):
                base = kind * (TEXT + quarter)
                ref[xl, base : base + TEXT, :] = text_ref[0, kind, :, head_columns(i)]
                ref[xl, base + TEXT : base + TEXT + quarter, :] = text_ref[
                    0, kind, i * quarter : (i + 1) * quarter, head_columns(4)
                ]

    @pl.when(core_ref[0] == 0)
    def _():
        write(keep_ref, 0)
        write(send_ref, 1)

    @pl.when(core_ref[0] != 0)
    def _():
        write(keep_ref, 1)
        write(send_ref, 0)


def scaled_queries(queries):
    scaled = queries.astype(F32) * SCALE
    high = scaled.astype(BF16)
    low = (scaled - high.astype(F32)).astype(BF16)
    return jnp.concatenate([high, low], axis=1)


def products(queries, keys):
    return lax.dot_general(queries, keys, (((1,), (1,)), ((), ())), preferred_element_type=F32)


def twice(keys):
    return jnp.concatenate([keys, keys], axis=1)


def with_ones(values):
    return jnp.concatenate([values, jnp.ones_like(values)], axis=1)


def fold(scores, values, state):
    top = jnp.max(scores, axis=1, keepdims=True)
    if state is not None:
        top = jnp.maximum(top, state[0])
    weights = jnp.exp2(scores - top).astype(BF16)
    summed = jnp.dot(weights, values, preferred_element_type=F32)
    total, summed = summed[:, HD : HD + 1], summed[:, :HD]
    if state is not None:
        shrink = jnp.exp2(state[0] - top)
        total = total + state[1] * shrink
        summed = summed + state[2] * shrink
    return top, total, summed


def write_result(out_ref, to, whole, part):
    count = to.size
    out_ref[to, 0:32, :] = (whole[2] / whole[1]).astype(BF16).reshape(count, ROWS, HD)
    out_ref[to, 32:64, :] = (part[2] / part[1]).astype(BF16).reshape(count, ROWS, HD)
    size = part[0] + jnp.log2(part[1])
    size = jnp.broadcast_to(size, (count * ROWS, HD))
    high = size.astype(BF16).astype(F32)
    middle = (size - high).astype(BF16).astype(F32)
    low = size - high - middle
    lane = lax.broadcasted_iota(jnp.int32, (count * ROWS, HD), 1)
    row = lax.broadcasted_iota(jnp.int32, (count * ROWS, HD), 0)
    terms = jnp.where(lane < 32, high, jnp.where(lane < 64, middle, low))
    terms = jnp.where((lane % 32 == row % 32) & (lane < 96), terms, 0.0)
    terms = jnp.sum(terms.reshape(count, ROWS, HD), axis=1, keepdims=True)
    out_ref[to, 64:80, :] = jnp.broadcast_to(terms, (count, 16, HD)).astype(BF16)


def fold_lazily(scaled, keys, values, state):
    top, total, summed = state
    for at in range(0, keys.shape[0], CHUNK):
        part = slice(at, min(at + CHUNK, keys.shape[0]))
        weights = jnp.exp2(products(scaled, keys[part]) - top).astype(BF16)
        term = jnp.dot(weights, values[part], preferred_element_type=F32)
        total = total + term[:, HD : HD + 1]
        summed = summed + term[:, :HD]
    return top, total, summed


SENDERS = 8
CHUNK = 512
MOST = 2.0**64


def keys_and_values(shard_refs):
    keys, values, part_keys, part_values = [], [], [], []
    for ref in shard_refs:
        count = ref.shape[0]
        keys.append(ref[:, 0:32, :].reshape(count * 32, HD))
        values.append(ref[:, 32:64, :].reshape(count * 32, HD))
        quarter = ref[:, 64:80, :].astype(F32)
        part_keys.append(quarter[:, 0:8].reshape(count * 8, HD).astype(BF16))
        part_values.append(quarter[:, 8:16].reshape(count * 8, HD).astype(BF16))
    return (
        (twice(jnp.concatenate(keys)), with_ones(jnp.concatenate(values))),
        (twice(jnp.concatenate(part_keys)), with_ones(jnp.concatenate(part_values))),
    )


def self_kernel(shards, first, last, *refs):
    queries_ref, shard_refs, rest = refs[0], refs[1 : 1 + shards], refs[1 + shards :]
    if not first:
        whole_ref, part_ref, stats_ref = rest[:3]
        rest = rest[3:]
    block = SENDERS * ROWS

    def queries_of(senders):
        return [scaled_queries(queries_ref[senders, at : at + 32, :].reshape(block, HD)) for at in (0, 32)]

    def states_of(rows):
        stats = stats_ref[rows]
        return (stats[:, 0:1], stats[:, 1:2], whole_ref[rows]), (stats[:, 2:3], stats[:, 3:4], part_ref[rows])

    def write(senders, rows, whole, part):
        if last:
            write_result(rest[0], senders, whole, part)
            return
        whole_out, part_out, stats_out = rest
        whole_out[rows] = whole[2]
        part_out[rows] = part[2]
        lane = lax.broadcasted_iota(jnp.int32, (block, HD), 1)
        stats_out[rows] = jnp.where(
            lane == 0, whole[0], jnp.where(lane == 1, whole[1], jnp.where(lane == 2, part[0], part[1]))
        )

    def places(index):
        start = index * block if isinstance(index, int) else pl.multiple_of(index * block, block)
        return pl.ds(index * SENDERS, SENDERS), pl.ds(start, block)

    pairs = keys_and_values(shard_refs)
    most = None
    for index in range(PEERS // SENDERS):
        senders, rows = places(index)
        scaled = queries_of(senders)
        if first:
            write(senders, rows, *(fold(products(q, k), v, None) for q, (k, v) in zip(scaled, pairs)))
            continue
        found = [fold_lazily(q, k, v, state) for q, (k, v), state in zip(scaled, pairs, states_of(rows))]
        write(senders, rows, *found)
        totals = jnp.maximum(found[0][1], found[1][1])
        most = totals if most is None else jnp.maximum(most, totals)
    if first:
        return

    @pl.when(jnp.max(most) > MOST)
    def _():
        again = keys_and_values(shard_refs)

        def redo(index, carry):
            senders, rows = places(index)
            found = [
                fold(products(q, k), v, state)
                for q, (k, v), state in zip(queries_of(senders), again, states_of(rows))
            ]
            write(senders, rows, *found)
            return carry

        lax.fori_loop(0, PEERS // SENDERS, redo, 0)


def self_step(queries, shards, state, last=False):
    first = state is None
    if last:
        out_shape = jax.ShapeDtypeStruct((PEERS, 80, HD), BF16)
    else:
        out_shape = [jax.ShapeDtypeStruct((PLANE_ROWS, HD), F32)] * 3
    keys = sum(s.shape[0] for s in shards) * 40
    cost = pl.CostEstimate(
        flops=4 * PLANE_ROWS * keys * HD * 2,
        bytes_accessed=keys * HD * 4 + PLANE_ROWS * HD * 16,
        transcendentals=PLANE_ROWS * keys,
    )
    operands = (queries, *shards, *(() if first else state))
    kernel = functools.partial(self_kernel, len(shards), first, last)
    return call(kernel, out_shape, operands, cost, specs=[query_rows()])


def cross_kernel(scalars_ref, queries_ref, text_ref, out_ref):
    length, place = scalars_ref[0], scalars_ref[1]
    quarter = TEXT // SPLIT
    block = SENDERS * ROWS

    def masked(scores, start):
        at = start + lax.broadcasted_iota(jnp.int32, scores.shape, 1)
        return jnp.where(at < length, scores, -1e30)

    keys, part_keys = twice(text_ref[0:512, :]), twice(text_ref[512:640, :])
    values, part_values = with_ones(text_ref[640:1152, :]), with_ones(text_ref[1152:1280, :])
    for index in range(PEERS // SENDERS):
        senders = pl.ds(index * SENDERS, SENDERS)
        scaled = [scaled_queries(queries_ref[senders, at : at + 32, :].reshape(block, HD)) for at in (0, 32)]
        whole = fold(masked(products(scaled[0], keys), 0), values, None)
        part = fold(masked(products(scaled[1], part_keys), place * quarter), part_values, None)
        write_result(out_ref, senders, whole, part)


def cross_step(scalars, queries, text):
    cost = pl.CostEstimate(
        flops=4 * PLANE_ROWS * 640 * HD * 2, bytes_accessed=2 * 1024 * 1024, transcendentals=PLANE_ROWS * 640
    )
    out_shape = jax.ShapeDtypeStruct((PEERS, 80, HD), BF16)
    return call(cross_kernel, out_shape, (scalars, queries, text), cost, scalars=1, specs=[query_rows()])


def merged(message_ref, slot, j):
    lane = lax.broadcasted_iota(jnp.int32, (ROWS, HD), 1)
    row = lax.broadcasted_iota(jnp.int32, (ROWS, HD), 0)
    mine = (lane % 32 == row) & (lane < 96)
    sizes = []
    for i in range(SPLIT):
        terms = message_ref[slot(i, j), 64:80, :].astype(F32)[0:1]
        sizes.append(jnp.sum(jnp.where(mine, jnp.broadcast_to(terms, (ROWS, HD)), 0.0), axis=1, keepdims=True))
    top = functools.reduce(jnp.maximum, sizes)
    shares = [jnp.exp2(s - top) for s in sizes]
    summed = sum(
        share * message_ref[slot(i, j), 32:64, :].astype(F32) for i, share in enumerate(shares)
    )
    return (summed / sum(shares)).astype(BF16)


def unpack_kernel(slot, gated, *refs):
    message_ref, out_ref = refs[0], refs[-1]
    for j in range(GROUPS):
        for i in range(SPLIT + 1):
            columns = head_columns(5 * j + i)
            rows = message_ref[slot(i, j), 0:32, :] if i < SPLIT else merged(message_ref, slot, j)
            if gated:
                rows = (refs[1][0:1, columns] * rows.astype(F32)).astype(BF16)
            out_ref[:, columns] = rows


def unpack(slot, message, gate=None):
    operands = [message] if gate is None else [message, gate]
    out_shape = jax.ShapeDtypeStruct((ROWS, 40 * HD), BF16)
    return call(functools.partial(unpack_kernel, slot, gate is not None), out_shape, operands)


def exchange(messages, group):
    return lax.all_to_all(messages, group, split_axis=0, concat_axis=0, tiled=True)


def shift(block, by):
    pairs = [(RING_ORDER[x], RING_ORDER[(x + by) % 4]) for x in range(4)]
    return lax.ppermute(block, RING, pairs)


def swap(block, axis, distance=1):
    size = dict(zip(AXES, SIZES))[axis]
    return lax.ppermute(block, axis, [(at, at ^ distance) for at in range(size)])


def pick(block, index):
    return lax.dynamic_index_in_dim(block, index, 0, keepdims=False)


def text_of_plane(text_context, chosen):
    xl, core = lax.axis_index("xl"), lax.axis_index("core")
    part = jax.ShapeDtypeStruct((2, 1280, HD), BF16)
    keep, send = call(pack_text_kernel, [part, part], (core.reshape(1), text_context), scalars=1)
    held = jnp.where(chosen % 2 == core, keep, swap(send, "core"))
    return jnp.where(chosen // 2 % 2 == xl, pick(held, xl), swap(pick(held, 1 - xl), "xl"))


def text_along_z(held, distance, chosen):
    agrees = (lax.axis_index("z") ^ (chosen // 4)) & distance == 0
    return jnp.where(agrees, held, swap(held, "z", distance))


def on_device(
    self_queries,
    self_keys,
    self_values,
    text_queries,
    text_context,
    sample,
    text_lengths,
    timestep,
    time_gates,
):
    chosen = sample[0]
    barrier = lax.optimization_barrier
    def message(rows):
        return jax.ShapeDtypeStruct((PEERS, rows, HD), BF16)

    blocks = call(pack_kernel, message(144), (self_keys, self_values, self_queries))
    text_blocks = call(pack_queries_kernel, message(64), (text_queries,))
    text = text_of_plane(text_context, chosen)
    queries = exchange(blocks, COLUMN)
    queries, text_blocks, text = barrier((queries, text_blocks, text))
    own, text = barrier((queries[:, 64:144], text))
    half = PEERS // 2

    up, down, other = shift(own, 1), shift(own, -1), swap(own, "core")
    text = text_along_z(text, 4, chosen)
    state = self_step(queries, [own], None)
    cross_queries = exchange(text_blocks, PLANE)
    up, down, other, text, state = barrier((up, down, other, text, state))

    far = [shift(up[:half], 1), shift(down[half:], -1)]
    other_up, other_down = swap(up, "core"), swap(down, "core")
    text = text_along_z(text, 2, chosen)
    state = self_step(queries, [other, up, down], state)
    far, other_up, other_down, text, state, cross_queries = barrier(
        (far, other_up, other_down, text, state, cross_queries)
    )

    other_far = [swap(x, "core") for x in far]
    text = text_along_z(text, 1, chosen)
    state = self_step(queries, [other_up, other_down, *far], state)
    other_far, text, state = barrier((other_far, text, state))

    place = lax.axis_index("xl") * 2 + lax.axis_index("core")
    cross = cross_step(jnp.stack([pick(text_lengths, chosen), place]), cross_queries, text)
    cross = exchange(cross, PLANE)
    result = exchange(self_step(queries, other_far, state, last=True), COLUMN)
    gate = lax.dynamic_slice_in_dim(time_gates, pick(timestep, chosen), 1, 0)
    return (unpack(self_slot, result, gate), unpack(cross_slot, cross))


def solution(mesh):
    fine = Mesh(mesh.devices.reshape(SIZES), AXES)
    rows = P(AXES, None)
    in_specs = (rows, rows, rows, rows, P(AXES[:3], None, None, AXES[3:]), P(), P(), P(), P())
    return jax.shard_map(on_device, mesh=fine, in_specs=in_specs, out_specs=(rows, rows), check_vma=False)
```

```python
import functools
import math

import jax
import jax.numpy as jnp
from jax import lax
from jax.experimental import pallas as pl
from jax.experimental.pallas import tpu as pltpu
from jax.sharding import Mesh, PartitionSpec as P

AXES = ("z", "xl", "core", "xh", "y")
SIZES = (8, 2, 2, 2, 4)
PLANES = SIZES[0]
PLANE = ("xl", "core", "xh", "y")
COLUMN = ("z", "y")
RING = ("xl", "xh")
RING_ORDER = (0, 2, 1, 3)

HD = 128
ROWS = 32
GROUPS = 8
SPLIT = 4
PEERS = GROUPS * SPLIT
PLANE_ROWS = PEERS * ROWS
TEXT = 512
SCALE = math.log2(math.e) / math.sqrt(HD)
F32 = jnp.float32
BF16 = jnp.bfloat16
VMEM_LIMIT = 63 * 1024 * 1024


def whole_block(shape):
    return pl.BlockSpec(shape, lambda step: (0,) * len(shape))


def call(kernel, out_shape, operands, cost=None, scalars=0, specs=()):
    in_specs = [pl.BlockSpec(memory_space=pltpu.SMEM)] * scalars + list(specs)
    in_specs += [whole_block(x.shape) for x in operands[len(in_specs) :]]
    return pl.pallas_call(
        kernel,
        out_shape=out_shape,
        grid=(1,),
        in_specs=in_specs,
        out_specs=jax.tree.map(lambda x: whole_block(x.shape), out_shape),
        cost_estimate=cost,
        compiler_params=pltpu.CompilerParams(vmem_limit_bytes=VMEM_LIMIT),
    )(*operands)


def query_rows():
    return pl.BlockSpec((PEERS, 64, HD), lambda step: (0, 0, 0))


def head_columns(head):
    return slice(head * HD, (head + 1) * HD)


def self_slot(i, j):
    return j * SPLIT + i


def cross_slot(i, j):
    return i * GROUPS + j


def pack_kernel(keys_ref, values_ref, queries_ref, out_ref):
    quarter = ROWS // SPLIT
    for j in range(GROUPS):
        fifth = head_columns(5 * j + 4)
        key_rows = keys_ref[:, fifth].astype(F32)
        value_rows = values_ref[:, fifth].astype(F32)
        for i in range(SPLIT):
            to = self_slot(i, j)
            own = head_columns(5 * j + i)
            out_ref[to, 0:32, :] = queries_ref[:, own]
            out_ref[to, 32:64, :] = queries_ref[:, fifth]
            out_ref[to, 64:96, :] = keys_ref[:, own]
            out_ref[to, 96:128, :] = values_ref[:, own]
            part = slice(i * quarter, (i + 1) * quarter)
            out_ref[to, 128:144, :] = jnp.concatenate([key_rows[part], value_rows[part]]).astype(BF16)


def pack_queries_kernel(queries_ref, out_ref):
    for j in range(GROUPS):
        for i in range(SPLIT):
            to = cross_slot(i, j)
            out_ref[to, 0:32, :] = queries_ref[:, head_columns(5 * j + i)]
            out_ref[to, 32:64, :] = queries_ref[:, head_columns(5 * j + 4)]


def pack_text_kernel(core_ref, text_ref, keep_ref, send_ref):
    quarter = TEXT // SPLIT

    def write(ref, core):
        for xl in range(2):
            i = xl * 2 + core
            for kind in range(2):
                base = kind * (TEXT + quarter)
                ref[xl, base : base + TEXT, :] = text_ref[0, kind, :, head_columns(i)]
                ref[xl, base + TEXT : base + TEXT + quarter, :] = text_ref[
                    0, kind, i * quarter : (i + 1) * quarter, head_columns(4)
                ]

    @pl.when(core_ref[0] == 0)
    def _():
        write(keep_ref, 0)
        write(send_ref, 1)

    @pl.when(core_ref[0] != 0)
    def _():
        write(keep_ref, 1)
        write(send_ref, 0)


def scaled_queries(queries):
    scaled = queries.astype(F32) * SCALE
    high = scaled.astype(BF16)
    low = (scaled - high.astype(F32)).astype(BF16)
    return jnp.concatenate([high, low], axis=1)


def products(queries, keys):
    return lax.dot_general(queries, keys, (((1,), (1,)), ((), ())), preferred_element_type=F32)


def twice(keys):
    return jnp.concatenate([keys, keys], axis=1)


def with_ones(values):
    return jnp.concatenate([values, jnp.ones_like(values)], axis=1)


def fold(scores, values, state):
    top = jnp.max(scores, axis=1, keepdims=True)
    if state is not None:
        top = jnp.maximum(top, state[0])
    weights = jnp.exp2(scores - top).astype(BF16)
    summed = jnp.dot(weights, values, preferred_element_type=F32)
    total, summed = summed[:, HD : HD + 1], summed[:, :HD]
    if state is not None:
        shrink = jnp.exp2(state[0] - top)
        total = total + state[1] * shrink
        summed = summed + state[2] * shrink
    return top, total, summed


def write_result(out_ref, to, whole, part):
    count = to.size
    out_ref[to, 0:32, :] = (whole[2] / whole[1]).astype(BF16).reshape(count, ROWS, HD)
    out_ref[to, 32:64, :] = (part[2] / part[1]).astype(BF16).reshape(count, ROWS, HD)
    size = part[0] + jnp.log2(part[1])
    size = jnp.broadcast_to(size, (count * ROWS, HD))
    high = size.astype(BF16).astype(F32)
    middle = (size - high).astype(BF16).astype(F32)
    low = size - high - middle
    lane = lax.broadcasted_iota(jnp.int32, (count * ROWS, HD), 1)
    row = lax.broadcasted_iota(jnp.int32, (count * ROWS, HD), 0)
    terms = jnp.where(lane < 32, high, jnp.where(lane < 64, middle, low))
    terms = jnp.where((lane % 32 == row % 32) & (lane < 96), terms, 0.0)
    terms = jnp.sum(terms.reshape(count, ROWS, HD), axis=1, keepdims=True)
    out_ref[to, 64:80, :] = jnp.broadcast_to(terms, (count, 16, HD)).astype(BF16)


def fold_lazily(scaled, keys, values, state):
    top, total, summed = state
    for at in range(0, keys.shape[0], CHUNK):
        part = slice(at, min(at + CHUNK, keys.shape[0]))
        weights = jnp.exp2(products(scaled, keys[part]) - top).astype(BF16)
        term = jnp.dot(weights, values[part], preferred_element_type=F32)
        total = total + term[:, HD : HD + 1]
        summed = summed + term[:, :HD]
    return top, total, summed


SENDERS = 8
CHUNK = 512
MOST = 2.0**64


def keys_and_values(shard_refs):
    keys, values, part_keys, part_values = [], [], [], []
    for ref in shard_refs:
        count = ref.shape[0]
        keys.append(ref[:, 0:32, :].reshape(count * 32, HD))
        values.append(ref[:, 32:64, :].reshape(count * 32, HD))
        quarter = ref[:, 64:80, :].astype(F32)
        part_keys.append(quarter[:, 0:8].reshape(count * 8, HD).astype(BF16))
        part_values.append(quarter[:, 8:16].reshape(count * 8, HD).astype(BF16))
    return (
        (twice(jnp.concatenate(keys)), with_ones(jnp.concatenate(values))),
        (twice(jnp.concatenate(part_keys)), with_ones(jnp.concatenate(part_values))),
    )


def self_kernel(shards, first, last, *refs):
    queries_ref, shard_refs, rest = refs[0], refs[1 : 1 + shards], refs[1 + shards :]
    if not first:
        whole_ref, part_ref, stats_ref = rest[:3]
        rest = rest[3:]
    block = SENDERS * ROWS

    def queries_of(senders):
        return [scaled_queries(queries_ref[senders, at : at + 32, :].reshape(block, HD)) for at in (0, 32)]

    def states_of(rows):
        stats = stats_ref[rows]
        return (stats[:, 0:1], stats[:, 1:2], whole_ref[rows]), (stats[:, 2:3], stats[:, 3:4], part_ref[rows])

    def write(senders, rows, whole, part):
        if last:
            write_result(rest[0], senders, whole, part)
            return
        whole_out, part_out, stats_out = rest
        whole_out[rows] = whole[2]
        part_out[rows] = part[2]
        lane = lax.broadcasted_iota(jnp.int32, (block, HD), 1)
        stats_out[rows] = jnp.where(
            lane == 0, whole[0], jnp.where(lane == 1, whole[1], jnp.where(lane == 2, part[0], part[1]))
        )

    def places(index):
        start = index * block if isinstance(index, int) else pl.multiple_of(index * block, block)
        return pl.ds(index * SENDERS, SENDERS), pl.ds(start, block)

    pairs = keys_and_values(shard_refs)
    most = None
    for index in range(PEERS // SENDERS):
        senders, rows = places(index)
        scaled = queries_of(senders)
        if first:
            write(senders, rows, *(fold(products(q, k), v, None) for q, (k, v) in zip(scaled, pairs)))
            continue
        found = [fold_lazily(q, k, v, state) for q, (k, v), state in zip(scaled, pairs, states_of(rows))]
        write(senders, rows, *found)
        totals = jnp.maximum(found[0][1], found[1][1])
        most = totals if most is None else jnp.maximum(most, totals)
    if first:
        return

    @pl.when(jnp.max(most) > MOST)
    def _():
        again = keys_and_values(shard_refs)

        def redo(index, carry):
            senders, rows = places(index)
            found = [
                fold(products(q, k), v, state)
                for q, (k, v), state in zip(queries_of(senders), again, states_of(rows))
            ]
            write(senders, rows, *found)
            return carry

        lax.fori_loop(0, PEERS // SENDERS, redo, 0)


def self_step(queries, shards, state, last=False):
    first = state is None
    if last:
        out_shape = jax.ShapeDtypeStruct((PEERS, 80, HD), BF16)
    else:
        out_shape = [jax.ShapeDtypeStruct((PLANE_ROWS, HD), F32)] * 3
    keys = sum(s.shape[0] for s in shards) * 40
    cost = pl.CostEstimate(
        flops=4 * PLANE_ROWS * keys * HD * 2,
        bytes_accessed=keys * HD * 4 + PLANE_ROWS * HD * 16,
        transcendentals=PLANE_ROWS * keys,
    )
    operands = (queries, *shards, *(() if first else state))
    kernel = functools.partial(self_kernel, len(shards), first, last)
    return call(kernel, out_shape, operands, cost, specs=[query_rows()])


def cross_kernel(scalars_ref, queries_ref, text_ref, out_ref):
    length, place = scalars_ref[0], scalars_ref[1]
    quarter = TEXT // SPLIT
    block = SENDERS * ROWS

    def masked(scores, start):
        at = start + lax.broadcasted_iota(jnp.int32, scores.shape, 1)
        return jnp.where(at < length, scores, -1e30)

    keys, part_keys = twice(text_ref[0:512, :]), twice(text_ref[512:640, :])
    values, part_values = with_ones(text_ref[640:1152, :]), with_ones(text_ref[1152:1280, :])
    for index in range(PEERS // SENDERS):
        senders = pl.ds(index * SENDERS, SENDERS)
        scaled = [scaled_queries(queries_ref[senders, at : at + 32, :].reshape(block, HD)) for at in (0, 32)]
        whole = fold(masked(products(scaled[0], keys), 0), values, None)
        part = fold(masked(products(scaled[1], part_keys), place * quarter), part_values, None)
        write_result(out_ref, senders, whole, part)


def cross_step(scalars, queries, text):
    cost = pl.CostEstimate(
        flops=4 * PLANE_ROWS * 640 * HD * 2, bytes_accessed=2 * 1024 * 1024, transcendentals=PLANE_ROWS * 640
    )
    out_shape = jax.ShapeDtypeStruct((PEERS, 80, HD), BF16)
    return call(cross_kernel, out_shape, (scalars, queries, text), cost, scalars=1, specs=[query_rows()])


def merged(message_ref, slot, j):
    lane = lax.broadcasted_iota(jnp.int32, (ROWS, HD), 1)
    row = lax.broadcasted_iota(jnp.int32, (ROWS, HD), 0)
    mine = (lane % 32 == row) & (lane < 96)
    sizes = []
    for i in range(SPLIT):
        terms = message_ref[slot(i, j), 64:80, :].astype(F32)[0:1]
        sizes.append(jnp.sum(jnp.where(mine, jnp.broadcast_to(terms, (ROWS, HD)), 0.0), axis=1, keepdims=True))
    top = functools.reduce(jnp.maximum, sizes)
    shares = [jnp.exp2(s - top) for s in sizes]
    summed = sum(
        share * message_ref[slot(i, j), 32:64, :].astype(F32) for i, share in enumerate(shares)
    )
    return (summed / sum(shares)).astype(BF16)


def unpack_kernel(slot, gated, *refs):
    message_ref, out_ref = refs[0], refs[-1]
    for j in range(GROUPS):
        for i in range(SPLIT + 1):
            columns = head_columns(5 * j + i)
            rows = message_ref[slot(i, j), 0:32, :] if i < SPLIT else merged(message_ref, slot, j)
            if gated:
                rows = (refs[1][0:1, columns] * rows.astype(F32)).astype(BF16)
            out_ref[:, columns] = rows


def unpack(slot, message, gate=None):
    operands = [message] if gate is None else [message, gate]
    out_shape = jax.ShapeDtypeStruct((ROWS, 40 * HD), BF16)
    return call(functools.partial(unpack_kernel, slot, gate is not None), out_shape, operands)


def exchange(messages, group):
    return lax.all_to_all(messages, group, split_axis=0, concat_axis=0, tiled=True)


def shift(block, by):
    pairs = [(RING_ORDER[x], RING_ORDER[(x + by) % 4]) for x in range(4)]
    return lax.ppermute(block, RING, pairs)


def swap(block, axis, distance=1):
    size = dict(zip(AXES, SIZES))[axis]
    return lax.ppermute(block, axis, [(at, at ^ distance) for at in range(size)])


def pick(block, index):
    return lax.dynamic_index_in_dim(block, index, 0, keepdims=False)


def text_of_plane(text_context, chosen):
    xl, core = lax.axis_index("xl"), lax.axis_index("core")
    part = jax.ShapeDtypeStruct((2, 1280, HD), BF16)
    keep, send = call(pack_text_kernel, [part, part], (core.reshape(1), text_context), scalars=1)
    held = jnp.where(chosen % 2 == core, keep, swap(send, "core"))
    return jnp.where(chosen // 2 % 2 == xl, pick(held, xl), swap(pick(held, 1 - xl), "xl"))


def text_along_z(held, distance, chosen):
    agrees = (lax.axis_index("z") ^ (chosen // 4)) & distance == 0
    return jnp.where(agrees, held, swap(held, "z", distance))


def on_device(
    self_queries,
    self_keys,
    self_values,
    text_queries,
    text_context,
    sample,
    text_lengths,
    timestep,
    time_gates,
):
    chosen = sample[0]
    barrier = lax.optimization_barrier
    def message(rows):
        return jax.ShapeDtypeStruct((PEERS, rows, HD), BF16)

    blocks = call(pack_kernel, message(144), (self_keys, self_values, self_queries))
    text_blocks = call(pack_queries_kernel, message(64), (text_queries,))
    text = text_of_plane(text_context, chosen)
    queries = exchange(blocks, COLUMN)
    queries, text_blocks, text = barrier((queries, text_blocks, text))
    own, text = barrier((queries[:, 64:144], text))

    up, down, other = shift(own, 1), shift(own, -1), swap(own, "core")
    text = text_along_z(text, 4, chosen)
    state = self_step(queries, [own], None)
    cross_queries = exchange(text_blocks, PLANE)
    up, down, other, text, state = barrier((up, down, other, text, state))

    far = shift(up, 1)
    other_up, other_down = swap(up, "core"), swap(down, "core")
    text = text_along_z(text, 2, chosen)
    state = self_step(queries, [other, up, down], state)
    far, other_up, other_down, text, state, cross_queries = barrier(
        (far, other_up, other_down, text, state, cross_queries)
    )

    other_far = swap(far, "core")
    text = text_along_z(text, 1, chosen)
    state = self_step(queries, [other_up, other_down], state)
    other_far, text, state = barrier((other_far, text, state))

    place = lax.axis_index("xl") * 2 + lax.axis_index("core")
    cross = cross_step(jnp.stack([pick(text_lengths, chosen), place]), cross_queries, text)
    cross = exchange(cross, PLANE)
    result = exchange(self_step(queries, [far, other_far], state, last=True), COLUMN)
    gate = lax.dynamic_slice_in_dim(time_gates, pick(timestep, chosen), 1, 0)
    return (unpack(self_slot, result, gate), unpack(cross_slot, cross))


def solution(mesh):
    fine = Mesh(mesh.devices.reshape(SIZES), AXES)
    rows = P(AXES, None)
    in_specs = (rows, rows, rows, rows, P(AXES[:3], None, None, AXES[3:]), P(), P(), P(), P())
    return jax.shard_map(on_device, mesh=fine, in_specs=in_specs, out_specs=(rows, rows), check_vma=False)
```
